32 devices in a mesh: img: 8 (over y, x, core), pw: 4 (over z).
Axes of the slice: x: 2, y: 2, z: 4, core: 2. Of those that a mesh axis runs over, the one named last changes fastest.
Arguments:
- band_panel: bfloat16 [1024, 57344], P(None, 'pw'), may hold values from -0.0793431812 to 0.0793431812
- gsphere: int32 [57344], P('pw'), may hold values from 0 to 65535, as said below
- eps_band: float32 [2], replicated, may hold values from -2 to -0.5
- local_pot: float32 [64, 4096], P('pw'), may hold values from 0.5 to 3
- dvpert: bfloat16 [128, 64, 4096], P('img', 'pw'), may hold values from -6 to 6
- beta_proj: float32 [4096, 128], P('pw'), may hold values from -1.5 to 1.5
- proj_coef: float32 [4096], P('pw'), may hold values from 0.5 to 2
- pblock: int32 [4096], P('pw'), may hold values from 0 to 511
Outputs:
- density_resp: float32 [128, 64, 4096], P('img', 'pw')
- chi_matrix: float32 [128, 128], P(None, 'img')
The draws below stay inside these ranges and needn't reach their ends.
Inputs may be any that keep to these rules, and one draw needn't show every extreme that they name: `gsphere`: each group of 14336 consecutive entries names distinct cells of the frequency slab of 64 x 16 x 64 cells of that group, in ascending order, always including its first and last cell. `pblock`: entry p counts blocks of 128 cells from the start of the grid slab of group p // 1024.
All inputs are finite; a program needn't handle non-finite values.
Results may differ from the reference program's by a relative error of at most 0.0035.
The reference program's roundings to bfloat16 on the way (of `over_b`) count: a program that leaves them out, or rounds other values in their place, can miss the bound.
Values may be sent and summed in bfloat16 or wider, within the bound.
A program may use at most 192 MiB of HBM per device.

```python
import math
import jax
import jax.numpy as jnp
from jax import lax

N = 64
NOCC = 1024
NPW = 57344
NPERT = 128
NB = 2
ITERS = 2
PROJ = 4096
BLEN = 128
BLOCKS_DEV = 512
N_PW = 4


def draw_band_panel(key, part):
    key = jax.random.fold_in(key, 23)
    row_key, entry_key = jax.random.split(key)
    limit = 19.0 / NPW ** 0.5
    spread = jax.random.uniform(row_key, (NOCC, 1), jnp.float32)
    entries = jax.random.normal(entry_key, (NOCC, NPW), jnp.float32)
    amplitude = 1.5 * jnp.exp(spread * (0.5 * math.log(10.0)))
    values = amplitude * entries / NPW ** 0.5
    return jnp.clip(values, -limit, limit).astype(jnp.bfloat16)


def draw_gsphere(key, part):
    key = jax.random.fold_in(key, 11)
    cells_dev = N * N * N // N_PW
    chosen = NPW // N_PW

    def one_device(device):
        dev_key = jax.random.fold_in(key, device)
        interior = jax.random.permutation(dev_key, cells_dev - 2)[:chosen - 2].astype(jnp.int32) + 1
        first_cell = jnp.zeros((1,), jnp.int32)
        last_cell = jnp.full((1,), cells_dev - 1, jnp.int32)
        return jnp.sort(jnp.concatenate([first_cell, interior, last_cell]))
    return lax.map(one_device, jnp.arange(N_PW, dtype=jnp.int32)).reshape(NPW)


def place_ends(drawn, own_key, smallest, largest):
    place = [jax.random.randint(jax.random.fold_in(own_key, axis), (), 0, length) for axis, length in enumerate(drawn.shape)]
    widest = drawn.shape.index(max(drawn.shape))
    beside = place[:widest] + [(place[widest] + 1) % drawn.shape[widest]] + place[widest + 1:]
    return drawn.at[tuple(place)].set(smallest).at[tuple(beside)].set(largest)


def shard_levels(rng, dims, cuts, smallest, largest):
    gain, own = 1.0, jax.random.fold_in(rng, 6)
    for axis_at, parts in cuts:
        heights = jnp.exp(jax.random.uniform(jax.random.fold_in(own, axis_at), (parts,), jnp.float32, smallest / len(cuts), largest / len(cuts)))
        gain = gain * jnp.repeat(heights, dims[axis_at] // parts).reshape([-1 if axis == axis_at else 1 for axis in range(len(dims))])
    return gain


def scatter_about(rng, dims, scale, most, pieces=(), held_as=jnp.bfloat16):
    values = jax.random.normal(rng, dims, jnp.float32) * scale
    if len(pieces) > 0:
        values = shard_levels(rng, dims, pieces, -0.22, 0.18) * values
    return jnp.clip(values, min=-most, max=most).astype(held_as)


def setup_inputs(seed: int = 0) -> dict:
    splits = jax.random.split(jax.random.key(seed), 9)
    band_panel = draw_band_panel(jax.random.fold_in(splits[8], 71), 0)
    gsphere = draw_gsphere(jax.random.fold_in(splits[8], 71), 0)
    eps_band = jnp.clip(jax.random.uniform(splits[2], (NB,), jnp.float32, -2.0, -0.5), -2.0, -0.5)
    local_pot = jnp.clip(0.5 + 2.5 * jax.random.uniform(splits[3], (N, N * N), jnp.float32) ** shard_levels(splits[3], (N, N * N), ((0, 4),), -0.2, 0.2), 0.5, 3.0)
    dvpert = scatter_about(splits[4], (NPERT, N, N * N), 1.0, 6.0, ((0, 8), (1, 4)))
    beta_proj = scatter_about(splits[5], (PROJ, BLEN), 0.25, 1.5, ((0, 4),), jnp.float32)
    proj_coef = jnp.clip(jnp.exp(math.log(2.0) - 1.3862944 * jax.random.uniform(splits[6], (PROJ,), jnp.float32) ** shard_levels(splits[6], (PROJ,), ((0, 4),), -0.2, 0.2)), 0.5, 2.0)
    pblock = place_ends(jax.random.randint(splits[7], (PROJ,), 0, BLOCKS_DEV), jax.random.fold_in(splits[7], 1), 0, BLOCKS_DEV - 1).astype(jnp.int32)
    return {"band_panel": band_panel, "gsphere": gsphere, "eps_band": eps_band, "local_pot": local_pot, "dvpert": dvpert, "beta_proj": beta_proj, "proj_coef": proj_coef, "pblock": pblock}


ALPHA_PV = 2.0
SHIFT_EPS = 1e-6
HIGHEST = lax.Precision.HIGHEST


def cas_table(length):
    idx_line = jnp.arange(length, dtype=jnp.int32)
    product = (idx_line[:, None] * idx_line[None, :]) % length
    angle = product.astype(jnp.float32) * (2.0 * math.pi / length)
    return jnp.cos(angle) + jnp.sin(angle)


def frequency(index_vals, length):
    return jnp.where(index_vals < length // 2, index_vals, index_vals - length).astype(jnp.float32)


def reference(band_panel, gsphere, eps_band, local_pot, dvpert, beta_proj, proj_coef, pblock):
    cas_rows = cas_table(N)
    slab_rows = N // N_PW
    owner_dev = jnp.arange(NPW, dtype=jnp.int32) // (NPW // N_PW)
    freq_x = gsphere // (slab_rows * N)
    freq_y = owner_dev * slab_rows + (gsphere // N) % slab_rows
    freq_z = gsphere % N
    box_index = (freq_x * N + freq_y) * N + freq_z
    kx_val = frequency(freq_x, N)
    ky_val = frequency(freq_y, N)
    kz_val = frequency(freq_z, N)
    kinetic = 8.0 * (kx_val * kx_val + ky_val * ky_val + kz_val * kz_val) / (N * N)
    proj_dev = PROJ // N_PW
    blocks_dev = N * N * N // (BLEN * N_PW)
    proj_block = (jnp.arange(PROJ, dtype=jnp.int32) // proj_dev) * blocks_dev + pblock

    def to_real(coeffs):
        batch_size = coeffs.shape[0]
        whole_box = jnp.zeros((batch_size, N * N * N), coeffs.dtype).at[:, box_index].set(coeffs)
        whole_box = whole_box.reshape(batch_size, N, N, N)
        result = jnp.einsum("wabc,ax->wxbc", whole_box, cas_rows, precision=HIGHEST)
        result = jnp.einsum("wxbc,by->wxyc", result, cas_rows, precision=HIGHEST)
        result = jnp.einsum("wxyc,cz->wxyz", result, cas_rows, precision=HIGHEST)
        return result.reshape(batch_size, N, N * N)

    def to_sphere(field_in):
        batch_size = field_in.shape[0]
        cube_cells = field_in.reshape(batch_size, N, N, N)
        result = jnp.einsum("wxyz,xa->wayz", cube_cells, cas_rows, precision=HIGHEST)
        result = jnp.einsum("wayz,yb->wabz", result, cas_rows, precision=HIGHEST)
        result = jnp.einsum("wabz,zc->wabc", result, cas_rows, precision=HIGHEST)
        result = result / (N * N * N)
        return result.reshape(batch_size, N * N * N)[:, box_index]

    def nonlocal_term(field_in):
        batch_size = field_in.shape[0]
        blocks = field_in.reshape(batch_size, N * N * N // BLEN, BLEN)
        picked = blocks[:, proj_block, :]
        proj_amp = jnp.sum(picked * beta_proj[None], axis=2) * proj_coef[None]
        addition = proj_amp[:, :, None] * beta_proj[None]
        return jnp.zeros_like(blocks).at[:, proj_block, :].add(addition).reshape(field_in.shape)

    def occupied(coeffs):
        correlation = jnp.dot(coeffs.astype(jnp.bfloat16), band_panel.T, preferred_element_type=jnp.float32)
        over_b = correlation.astype(jnp.bfloat16)
        back = jnp.dot(over_b, band_panel, preferred_element_type=jnp.float32)
        return back, correlation, over_b

    def apply_ham(coeffs):
        field_real = to_real(coeffs)
        potential = local_pot[None] * field_real + nonlocal_term(field_real)
        return kinetic[None] * coeffs + to_sphere(potential)

    bands_real = to_real(band_panel[:NB].astype(jnp.float32))

    def solve_one(perturb):
        products = perturb.astype(jnp.float32)[None] * bands_real
        source = to_sphere(products)
        back, correlation, over_b = occupied(source)
        right_side = back - source
        solution = jnp.zeros_like(right_side)
        residual = right_side
        direction = right_side
        norm_now = jnp.sum(residual * residual, axis=1)
        for iteration in range(ITERS):
            shifted = apply_ham(direction) - eps_band[:, None] * direction
            back, correlation, over_b = occupied(direction)
            curvature = jnp.sum(direction * shifted, axis=1) + ALPHA_PV * jnp.sum(correlation * over_b.astype(jnp.float32), axis=1)
            product_vec = shifted + ALPHA_PV * back
            step_len = norm_now / curvature
            solution = solution + step_len[:, None] * direction
            residual = residual - step_len[:, None] * product_vec
            if iteration + 1 < ITERS:
                norm_next = jnp.sum(residual * residual, axis=1)
                direction = residual + (norm_next / (norm_now + SHIFT_EPS))[:, None] * direction
                norm_now = norm_next
        change = to_real(solution)
        return 4.0 * jnp.sum(bands_real * change, axis=0)

    density_resp = lax.map(solve_one, dvpert)
    flat_pert = dvpert.reshape(NPERT, N * N * N).astype(jnp.float32)
    flat_rho = density_resp.reshape(NPERT, N * N * N)
    chi_matrix = jnp.dot(flat_pert, flat_rho.T, precision=HIGHEST) / (N * N * N)
    return density_resp, chi_matrix
```

```python
import math

import jax
import jax.numpy as jnp
from jax import lax
from jax.experimental import pallas as pl
from jax.experimental.pallas import tpu as pltpu
from jax.sharding import PartitionSpec as P

N = 64
NB = 2
ITERS = 2


ALPHA_PV = 2.0
SHIFT_EPS = 1e-06
HIGHEST = lax.Precision.HIGHEST


def cas_table(length):
    idx_line = jnp.arange(length, dtype=jnp.int32)
    product = idx_line[:, None] * idx_line[None, :] % length
    angle = product.astype(jnp.float32) * (2.0 * math.pi / length)
    return jnp.cos(angle) + jnp.sin(angle)


def frequency(index_vals, length):
    return jnp.where(index_vals < length // 2, index_vals, index_vals - length).astype(jnp.float32)


def slab_plan(band_panel, gsphere, eps_band, local_pot, dvpert, beta_proj, proj_coef, pblock):
    points = N
    slab_rows = local_pot.shape[0]
    plane_size = points * points
    cas_rows = cas_table(points)
    scaled_rows = cas_rows / points
    pw_rank = lax.axis_index("pw")
    freq_x = gsphere // (slab_rows * points)
    freq_y = pw_rank * slab_rows + gsphere // points % slab_rows
    freq_z = gsphere % points
    kx_val = frequency(freq_x, points)
    ky_val = frequency(freq_y, points)
    kz_val = frequency(freq_z, points)
    kinetic = 8.0 * (kx_val * kx_val + ky_val * ky_val + kz_val * kz_val) / (points * points)

    def to_real(coeffs):
        batch_size = coeffs.shape[0]
        freq_box = (
            jnp.zeros((batch_size, points * slab_rows * points), jnp.float32)
            .at[:, gsphere]
            .set(coeffs)
        )
        freq_box = freq_box.reshape(batch_size, points, slab_rows, points)
        along_x = jnp.einsum("wgyz,gx->wxyz", freq_box, cas_rows, precision=HIGHEST)
        pieces = lax.all_to_all(along_x, "pw", split_axis=1, concat_axis=2, tiled=True)
        partial_value = jnp.einsum("wxgz,gy->wxyz", pieces, cas_rows, precision=HIGHEST)
        partial_value = jnp.einsum("wxyg,gz->wxyz", partial_value, cas_rows, precision=HIGHEST)
        return partial_value.reshape(pieces.shape[0], slab_rows, plane_size)

    def to_sphere(field_in):
        batch_size = field_in.shape[0]
        cube_cells = field_in.reshape(batch_size, slab_rows, points, points)
        partial_value = jnp.einsum("wxyz,yg->wxgz", cube_cells, scaled_rows, precision=HIGHEST)
        partial_value = jnp.einsum("wxgz,zh->wxgh", partial_value, scaled_rows, precision=HIGHEST)
        pieces = lax.all_to_all(partial_value, "pw", split_axis=2, concat_axis=1, tiled=True)
        whole_box = jnp.einsum("wxgh,xf->wfgh", pieces, scaled_rows, precision=HIGHEST)
        return whole_box.reshape(pieces.shape[0], points * slab_rows * points)[:, gsphere]

    def correlation_part(coeffs):
        return lax.dot_general(
            coeffs.astype(jnp.bfloat16),
            band_panel,
            (((1,), (1,)), ((), ())),
            preferred_element_type=jnp.float32,
        )

    def correlations(coeffs):
        return lax.psum(correlation_part(coeffs), "pw")

    def residual_norm(residual):
        return lax.psum(jnp.sum(residual * residual, axis=1), "pw")

    pert_dev = dvpert.shape[0]
    batch_rows = pert_dev * NB
    bands_real = to_real(band_panel[:NB].astype(jnp.float32))
    products = dvpert.astype(jnp.float32)[:, None] * bands_real[None]
    source = to_sphere(products.reshape(batch_rows, slab_rows, plane_size))
    source_over = correlations(source).astype(jnp.bfloat16)
    right_side = jnp.dot(source_over, band_panel, preferred_element_type=jnp.float32) - source
    eps_rows = jnp.tile(eps_band, pert_dev)
    solution = jnp.zeros_like(right_side)
    residual = right_side
    direction = right_side
    norm_now = residual_norm(residual)
    for iteration in range(ITERS):
        correlation = correlations(direction)
        field_real = to_real(direction)
        nonlocal_batch_size = field_real.shape[0]
        blocks = field_real.reshape(
            nonlocal_batch_size, slab_rows * plane_size // beta_proj.shape[1], beta_proj.shape[1]
        )
        picked = blocks[:, pblock, :]
        proj_amp = jnp.sum(picked * beta_proj[None], axis=2) * proj_coef[None]
        addition = proj_amp[:, :, None] * beta_proj[None]
        potential = local_pot[None] * field_real + jnp.zeros_like(blocks).at[:, pblock, :].add(
            addition
        ).reshape(field_real.shape)
        applied, field_real = (kinetic[None] * direction + to_sphere(potential), field_real)
        shifted = applied - eps_rows[:, None] * direction
        curvature = lax.psum(jnp.sum(direction * shifted, axis=1), "pw")
        over_b = correlation.astype(jnp.bfloat16)
        curvature = curvature + ALPHA_PV * jnp.sum(correlation * over_b.astype(jnp.float32), axis=1)
        product_vec = shifted + ALPHA_PV * jnp.dot(
            over_b, band_panel, preferred_element_type=jnp.float32
        )
        step_len = norm_now / curvature
        solution = solution + step_len[:, None] * direction
        residual = residual - step_len[:, None] * product_vec
        if iteration + 1 < ITERS:
            norm_next = residual_norm(residual)
            direction = residual + (norm_next / (norm_now + SHIFT_EPS))[:, None] * direction
            norm_now = norm_next
    change = to_real(solution)
    density_resp = 4.0 * jnp.sum(
        bands_real[None] * change.reshape(pert_dev, NB, slab_rows, plane_size), axis=1
    )
    flat_rho = density_resp.reshape(pert_dev, slab_rows * plane_size)
    shard_in = lax.all_gather(dvpert, "img", axis=0, tiled=True)
    values = shard_in.reshape(shard_in.shape[0], slab_rows * plane_size).astype(jnp.float32)
    block_vals = lax.dot_general(
        values,
        flat_rho,
        (((1,), (1,)), ((), ())),
        precision=HIGHEST,
        preferred_element_type=jnp.float32,
    )
    chi_matrix = lax.psum(block_vals, "pw") / (points * points * points)
    return (density_resp, chi_matrix)


SENT = jnp.bfloat16
MID = lax.Precision.HIGH


LANES = 128
STEP_X = 8
VMEM_BYTES = 40 * 1024 * 1024


def swap_lines(tile):
    rows, lanes = tile.shape
    turned = pltpu.roll(pltpu.roll(tile, rows // 2, 0), lanes // 2, 1)
    low_lane = lax.broadcasted_iota(jnp.int32, tile.shape, 1) < lanes // 2
    low_row = lax.broadcasted_iota(jnp.int32, tile.shape, 0) < rows // 2
    return jnp.where(low_lane == low_row, tile, turned)


def pick_lanes(tile, index):
    return jnp.take_along_axis(tile, index & (LANES - 1), axis=1, mode="promise_in_bounds")


def expand_kernel(base_ref, place_ref, coeffs_ref, out_ref):
    pairs = out_ref.shape[1]
    first = pl.program_id(0) * STEP_X

    def body(step, carry):
        x, pair = step // pairs, step % pairs
        base = pl.multiple_of(base_ref[first + x, pair], LANES)
        index = jnp.broadcast_to(place_ref[x, pl.ds(pair, 1), :], (8, LANES))
        head = pick_lanes(coeffs_ref[:, pl.ds(base, LANES)], index)
        tail = pick_lanes(coeffs_ref[:, pl.ds(base + LANES, LANES)], index)
        found = jnp.where(index < LANES, head, tail)
        out_ref[x, pair] = swap_lines(jnp.where(index < 0, 0.0, found))
        return carry

    lax.fori_loop(0, STEP_X * pairs, body, 0, unroll=8)


def compress_kernel(base_ref, block_ref, entry_ref, box_ref, out_ref):
    pairs = box_ref.shape[1]
    first = pl.program_id(0) * STEP_X

    def body(step, carry):
        x, pair = step // pairs, step % pairs
        base = pl.multiple_of(base_ref[first + x, pair], LANES)
        tile = swap_lines(box_ref[x, pair])
        for shift in (0, LANES):
            window = pl.ds(base + shift, LANES)
            index = entry_ref[:, window] - block_ref[first + x, pair] * LANES
            inside = (index >= 0) & (index < LANES)
            out_ref[:, window] = jnp.where(inside, pick_lanes(tile, index), out_ref[:, window])
        return carry

    lax.fori_loop(0, STEP_X * pairs, body, 0, unroll=4)


def expand(base, place, coeffs):
    points, pairs = base.shape
    return pl.pallas_call(
        expand_kernel,
        grid=(points // STEP_X,),
        in_specs=[
            pl.BlockSpec(memory_space=pltpu.SMEM),
            pl.BlockSpec((STEP_X, pairs, LANES), lambda i: (i, 0, 0)),
            pl.BlockSpec(coeffs.shape, lambda i: (0, 0)),
        ],
        out_specs=pl.BlockSpec((STEP_X, pairs, 8, LANES), lambda i: (i, 0, 0, 0)),
        out_shape=jax.ShapeDtypeStruct((points, pairs, 8, LANES), jnp.float32),
        compiler_params=pltpu.CompilerParams(vmem_limit_bytes=VMEM_BYTES),
    )(base, place, coeffs)


def compress(base, block, entries, box):
    points, pairs = base.shape
    return pl.pallas_call(
        compress_kernel,
        grid=(points // STEP_X,),
        in_specs=[
            pl.BlockSpec(memory_space=pltpu.SMEM),
            pl.BlockSpec(memory_space=pltpu.SMEM),
            pl.BlockSpec(entries.shape, lambda i: (0, 0)),
            pl.BlockSpec((STEP_X, pairs, 8, LANES), lambda i: (i, 0, 0, 0)),
        ],
        out_specs=pl.BlockSpec(entries.shape, lambda i: (0, 0)),
        out_shape=jax.ShapeDtypeStruct(entries.shape, jnp.float32),
        compiler_params=pltpu.CompilerParams(vmem_limit_bytes=VMEM_BYTES),
    )(base, block, entries, box)


def local(band_panel, gsphere, eps_band, local_pot, dvpert, beta_proj, proj_coef, pblock):
    ranks = lax.axis_size("pw")
    pert_dev = dvpert.shape[0]
    if pert_dev % ranks or pert_dev // ranks * NB != 8 or gsphere.shape[0] % LANES:
        return slab_plan(
            band_panel, gsphere, eps_band, local_pot, dvpert, beta_proj, proj_coef, pblock
        )
    points = N
    slab_rows = local_pot.shape[0]
    lanes = NB * points
    perts = pert_dev // ranks
    sphere_dev = gsphere.shape[0]
    cas_rows = cas_table(points)
    scaled_rows = cas_rows / points
    pw_rank = lax.axis_index("pw")
    kx_val = frequency(gsphere // (slab_rows * points), points)
    ky_val = frequency(pw_rank * slab_rows + gsphere // points % slab_rows, points)
    kz_val = frequency(gsphere % points, points)
    kinetic = 8.0 * (kx_val * kx_val + ky_val * ky_val + kz_val * kz_val) / (points * points)

    def gather_pw(value, axis=0):
        return lax.all_gather(value, "pw", axis=axis, tiled=True)

    slab_cells = points * slab_rows * points
    owner = jnp.arange(ranks, dtype=jnp.int32)[:, None]
    entry_count = ranks * sphere_dev
    slab_pairs = slab_rows * points // LANES
    all_pairs = ranks * slab_pairs
    rows = perts * points

    def by_x(value):
        value = value.reshape(ranks, points, slab_pairs, -1)
        return value.transpose(1, 0, 2, 3).reshape(points, all_pairs, -1)

    slab_count = slab_cells // LANES
    first_cells = jnp.arange(slab_count, dtype=jnp.int32) * LANES
    starts = jnp.sum((gsphere[None, :] < first_cells[:, None]).astype(jnp.int32), axis=1)
    bases = starts // LANES * LANES
    placed = (
        jnp.full((slab_cells,), -1, jnp.int32)
        .at[gsphere]
        .set(
            jnp.arange(sphere_dev, dtype=jnp.int32),
            unique_indices=True,
            indices_are_sorted=True,
        )
    ).reshape(slab_count, LANES)
    placed = jnp.where(placed < 0, -1, placed - bases[:, None])
    place = by_x(gather_pw(placed))
    base = by_x(gather_pw(bases).reshape(ranks, -1) + owner * sphere_dev)[:, :, 0]
    block = by_x(jnp.arange(ranks * slab_count, dtype=jnp.int32))[:, :, 0]
    entries = (gather_pw(gsphere).reshape(ranks, sphere_dev) + owner * slab_cells).reshape(1, -1)
    entries = jnp.pad(entries, ((0, 0), (0, 2 * LANES)), constant_values=-1)
    entries = jnp.broadcast_to(entries, (8, entry_count + 2 * LANES))
    all_pot = gather_pw(local_pot).reshape(points, points, 1, points)
    all_pot = jnp.tile(all_pot, (1, 1, perts, NB)).reshape(points, rows, lanes)
    all_beta = gather_pw(beta_proj)
    all_coef = gather_pw(proj_coef)
    lines = beta_proj.shape[1] // points
    slab_blocks = slab_rows * points // lines
    pick = gather_pw(pblock)
    proj_dev = pblock.shape[0]
    proj_block = (pick.reshape(ranks, proj_dev) + owner * slab_blocks).reshape(-1)
    beta_lines = jnp.tile(all_beta.reshape(-1, lines, 1, points), (1, 1, perts, NB))
    beta_lines = beta_lines.reshape(-1, lines * perts, lanes)
    one_hot = (
        pick.reshape(ranks, 1, proj_dev)
        == jnp.arange(slab_blocks, dtype=jnp.int32)[None, :, None]
    ).astype(jnp.bfloat16)

    def pair(matrix):
        return jnp.kron(jnp.eye(NB, dtype=jnp.float32), matrix)

    def each_pert(matrix, count):
        return jnp.kron(matrix, jnp.eye(count, dtype=jnp.float32))

    def box_of(coeffs):
        coeffs = jnp.pad(coeffs.astype(jnp.float32), ((0, 0), (0, 2 * LANES)))
        return expand(base, place, coeffs).reshape(points, rows, lanes)

    def to_real(box):
        count = box.shape[1] // points
        box = jnp.einsum("xsm,mn->xsn", box, pair(cas_rows), precision=MID)
        box = jnp.einsum("xsm,sg->xgm", box, each_pert(cas_rows, count), precision=MID)
        return jnp.einsum("xsm,xg->gsm", box, cas_rows, precision=MID)

    def to_sphere(field):
        box = jnp.einsum("xsm,xg->gsm", field, scaled_rows, precision=MID)
        box = jnp.einsum("xsm,sg->xgm", box, each_pert(scaled_rows, perts), precision=MID)
        box = jnp.einsum("xsm,mn->xsn", box, pair(scaled_rows), precision=MID)
        box = box.reshape(points, all_pairs, 8, LANES)
        return compress(base, block, entries, box)[:, :entry_count]

    def spread(coeffs):
        return lax.all_to_all(coeffs.astype(SENT), "pw", split_axis=0, concat_axis=1, tiled=True)

    def collect(coeffs):
        return lax.all_to_all(
            coeffs.astype(SENT), "pw", split_axis=1, concat_axis=0, tiled=True
        )

    def correlations(coeffs):
        part = lax.dot_general(
            coeffs.astype(jnp.bfloat16),
            band_panel,
            (((1,), (1,)), ((), ())),
            preferred_element_type=jnp.float32,
        )
        return lax.psum(part, "pw")

    def occupied(over_b):
        return jnp.dot(over_b, band_panel, preferred_element_type=jnp.float32)

    def residual_norm(residual):
        return lax.psum(jnp.sum(residual * residual, axis=1), "pw")

    same_band = pair(jnp.ones((points, points), jnp.float32))

    def nonlocal_term(field):
        picked = field.reshape(-1, lines * perts, lanes)[proj_block]
        amp = jnp.sum((picked * beta_lines).reshape(-1, lines, perts, lanes), axis=1)
        amp = jnp.einsum("qpm,mn->qpn", amp, same_band, precision=MID)
        amp = jnp.tile(amp * all_coef[:, None, None], (1, lines, 1))
        addition = (amp * beta_lines).reshape(ranks, proj_dev, lines * perts, lanes)
        high = addition.astype(jnp.bfloat16)
        low = (addition - high.astype(jnp.float32)).astype(jnp.bfloat16)
        added = sum(
            jnp.einsum("dbq,dqsm->dbsm", one_hot, part, preferred_element_type=jnp.float32)
            for part in (high, low)
        )
        return added.reshape(field.shape)

    first_bands = gather_pw(band_panel[:NB], axis=1)
    band_box = box_of(jnp.repeat(first_bands, perts, axis=0))
    band_box = band_box.reshape(points, points, perts, lanes)[:, :, 0]
    bands_real = to_real(band_box)
    every_band = jnp.repeat(bands_real, perts, axis=1)
    pert_whole = lax.all_to_all(dvpert, "pw", split_axis=0, concat_axis=1, tiled=True)
    pert_cells = pert_whole.reshape(perts, points, points, points).transpose(1, 2, 0, 3)
    pert_cells = jnp.tile(pert_cells.astype(jnp.float32), (1, 1, 1, NB))
    products = pert_cells.reshape(points, rows, lanes) * every_band
    sent_source = collect(to_sphere(products))
    source = sent_source.astype(jnp.float32)
    every_source = lax.all_gather(
        sent_source.astype(jnp.bfloat16), "img", axis=0, tiled=True
    )
    source_over = correlations(source).astype(jnp.bfloat16)
    right_side = occupied(source_over) - source
    eps_rows = jnp.tile(jnp.repeat(eps_band, perts), ranks)
    change = jnp.zeros_like(right_side)
    residual = right_side
    direction = right_side
    norm_now = residual_norm(residual)
    for iteration in range(ITERS):
        correlation = correlations(direction)
        field_real = to_real(box_of(spread(direction)))
        potential = all_pot * field_real + nonlocal_term(field_real)
        applied = collect(to_sphere(potential)).astype(jnp.float32)
        shifted = applied + (kinetic[None] - eps_rows[:, None]) * direction
        curvature = lax.psum(jnp.sum(direction * shifted, axis=1), "pw")
        over_b = correlation.astype(jnp.bfloat16)
        curvature = curvature + ALPHA_PV * jnp.sum(correlation * over_b.astype(jnp.float32), axis=1)
        product_vec = shifted + ALPHA_PV * occupied(over_b)
        step_len = norm_now / curvature
        change = change + step_len[:, None] * direction
        if iteration + 1 < ITERS:
            residual = residual - step_len[:, None] * product_vec
            norm_next = residual_norm(residual)
            direction = residual + (norm_next / (norm_now + SHIFT_EPS))[:, None] * direction
            norm_now = norm_next
    response = to_real(box_of(spread(change))) * every_band
    density = 4.0 * jnp.sum(response.reshape(points, points, perts, NB, points), axis=3)
    density = density.astype(SENT).transpose(2, 0, 1, 3)
    density = density.reshape(perts, points, points * points)
    density_resp = lax.all_to_all(density, "pw", split_axis=1, concat_axis=0, tiled=True)
    every_source = every_source.reshape(-1, NB, perts, sphere_dev)
    change_high = change.astype(jnp.bfloat16)
    change_low = (change - change_high.astype(jnp.float32)).astype(jnp.bfloat16)
    chi_part = sum(
        lax.dot_general(
            every_source[:, band].reshape(-1, sphere_dev),
            part.reshape(ranks, NB, perts, sphere_dev)[:, band].reshape(pert_dev, sphere_dev),
            (((1,), (1,)), ((), ())),
            preferred_element_type=jnp.float32,
        )
        for band in range(NB)
        for part in (change_high, change_low)
    )
    chi_matrix = 4.0 * lax.psum(chi_part, "pw")
    return (density_resp.astype(jnp.float32), chi_matrix)


def solution(mesh):
    return jax.shard_map(
        local,
        mesh=mesh,
        in_specs=(
            P(None, "pw"),
            P("pw"),
            P(),
            P("pw", None),
            P("img", "pw", None),
            P("pw", None),
            P("pw"),
            P("pw"),
        ),
        out_specs=(P("img", "pw", None), P(None, "img")),
        check_vma=False,
    )
```
